256 devices in a mesh: row: 8 (over z_hi, y), col: 32 (over z_lo, x, core).
Axes of the slice: x: 4, y: 4, z: 8 (z_hi: 2, z_lo: 4; z = z_hi * 4 + z_lo), core: 2. Of those that a mesh axis runs over, the one named last changes fastest.
Arguments:
- sigma_anc: float32 [16384, 16384], P('row', 'col'), as said below
- factor: float32 [2048, 16384], P('col', 'row'), may hold values from -0.046875 to 0.046875
- pattern: int32 [8, 64], replicated, may hold values 0 or 1
- base_var: float32 [2048], P('col'), may hold values from 0.5 to 2
Outputs:
- sigma_off: float32 [2048, 16384], P('col', 'row')
- variances: float32 [2048], P('col')
The draws below stay inside these ranges and needn't reach their ends.
Inputs may be any that keep to these rules, and one draw needn't show every extreme that they name: sigma_anc is exactly symmetric, with positive diagonal entries.
All inputs are finite; a program needn't handle non-finite values.
Results may differ from the reference program's by a relative error of at most 0.00007.
Values sent between devices are 32-bit elements; how exact they have to be, the bound alone decides.
No kernel may reach another device: no remote copies, remote signals or barrier semaphores. Data moves between devices by JAX's collectives and lax.ppermute only.
A program may use at most 64 MiB of HBM per device.

```python
import math
import jax
import jax.numpy as jnp
from jax import lax

B = 256
NA = 64
K = 8
M = 16384
KB = 2048


def draw_sigma_anc(key, part):
    key = jax.random.fold_in(key, 11)
    first, second = jax.random.split(key)
    normal_part = jax.random.normal(first, (M, M), jnp.float32)
    scales = jnp.exp(jax.random.uniform(second, (M,), jnp.float32, math.log(0.7), math.log(1.4)))
    sym_part = (normal_part + normal_part.T) * (0.7 / math.sqrt(M))
    positions = jnp.arange(M)
    identity = (positions[:, None] == positions[None, :]).astype(jnp.float32)
    return scales[:, None] * scales[None, :] * (sym_part + identity)


def touch_ends(entries, stream_key, least, top_value):
    spot = [jax.random.randint(jax.random.fold_in(stream_key, axis), (), 0, length) for axis, length in enumerate(entries.shape)]
    widest = entries.shape.index(max(entries.shape))
    beside = spot[:widest] + [(spot[widest] + 1) % entries.shape[widest]] + spot[widest + 1:]
    return entries.at[tuple(spot)].set(least).at[tuple(beside)].set(top_value)


def shard_levels(key, dims, pieces, least, high):
    def one(dim, shards_of):
        draws = jax.random.uniform(jax.random.fold_in(jax.random.fold_in(key, 6), dim), (shards_of,), jnp.float32, least / len(pieces), high / len(pieces))
        return jnp.repeat(jnp.exp(draws), dims[dim] // shards_of).reshape((-1,) + (1,) * (len(dims) - dim - 1))

    factor_of = one(*pieces[0])
    for cut in pieces[1:]:
        factor_of = factor_of * one(*cut)
    return factor_of


def scatter_about(stream_key, dims, scale, reach, cuts=(), dtype=jnp.bfloat16):
    result = scale * jax.random.normal(stream_key, dims, jnp.float32)
    if cuts:
        result = result * shard_levels(stream_key, dims, cuts, -0.22, 0.18)
    return jnp.clip(result, -reach, reach).astype(dtype)


def setup_inputs(seed: int = 0) -> dict:
    arg_keys = jax.random.split(jax.random.key(seed), 5)
    sigma_anc = draw_sigma_anc(jax.random.fold_in(arg_keys[4], 71), 0)
    factor = scatter_about(arg_keys[1], (KB, M), M ** -0.5, 0.046875, ((0, 32), (1, 8)), jnp.float32)
    pattern = touch_ends((jax.random.randint(arg_keys[2], (K, NA), 0, 2) < 1).astype(jnp.int32), jax.random.fold_in(arg_keys[2], 1), 0, 1)
    base_var = jnp.clip(jnp.exp(math.log(2.0) - 1.3862944 * jax.random.uniform(arg_keys[3], (KB,), jnp.float32) ** shard_levels(arg_keys[3], (KB,), ((0, 32),), -0.2, 0.2)), 0.5, 2.0)
    return {"sigma_anc": sigma_anc, "factor": factor, "pattern": pattern, "base_var": base_var}


def reference(sigma_anc, factor, pattern, base_var):
    mask = jnp.repeat(jnp.repeat(pattern, B, axis=0), B, axis=1).astype(jnp.float32)
    masked = factor * mask
    product = jnp.dot(masked, sigma_anc, precision=lax.Precision.HIGHEST, preferred_element_type=jnp.float32)
    sigma_off = -(product * mask)
    variances = base_var + jnp.sum(product * masked, axis=1)
    return sigma_off, variances
```

```python
import jax
import jax.numpy as jnp
from jax import lax
from jax.experimental import pallas as pl
from jax.experimental.pallas import tpu as pltpu
from jax.sharding import PartitionSpec as P

B = 256
AXES = ("row", "col")
FIRST = 40
F32, BF16 = jnp.float32, jnp.bfloat16


def table(move):
    perm = []
    for i in range(256):
        zh, y, zl, x, k = i >> 7, (i >> 5) & 3, (i >> 3) & 3, (i >> 1) & 3, i & 1
        zh, y, zl, x, k = move(zh, y, zl, x, k)
        perm.append((i, (zh << 7) | ((y % 4) << 5) | ((zl % 4) << 3) | ((x % 4) << 1) | k))
    return perm


def along_x(n):
    return table(lambda zh, y, zl, x, k: (zh, y, zl, x + n, k))


def along_y(n):
    return table(lambda zh, y, zl, x, k: (zh, y + n, zl, x, k))


def along_zl(n):
    return table(lambda zh, y, zl, x, k: (zh, y, zl + n, x, k))


OTHER_ZH = table(lambda zh, y, zl, x, k: (1 - zh, y, zl, x, k))
OTHER_CORE = table(lambda zh, y, zl, x, k: (zh, y, zl, x, 1 - k))


def regroup(n):
    perm = []
    for i in range(256):
        r, c = i >> 5, i & 31
        perm.append((i, (c // 4) * 32 + 4 * r + (c + n) % 4))
    return perm


def send(value, perm):
    return lax.ppermute(value, AXES, perm)


def tie(*values):
    return lax.optimization_barrier(values)


def split(value):
    high = value.astype(BF16)
    return high, (value - high.astype(F32)).astype(BF16)


def split_kernel(value_ref, high_ref, low_ref):
    high_ref[...], low_ref[...] = split(value_ref[...])


def split_all(value):
    spec = pl.BlockSpec((256, value.shape[1]), lambda i: (i, 0))
    return pl.pallas_call(
        split_kernel,
        grid=(value.shape[0] // 256,),
        in_specs=[spec],
        out_specs=[spec] * 2,
        out_shape=[jax.ShapeDtypeStruct(value.shape, BF16)] * 2,
        name="split_sigma",
    )(value)


def whole_kernel(tab_ref, rows_ref, sh_ref, sl_ref, out_ref):
    step = pl.program_id(0)
    blocks, rows, depth = rows_ref.shape
    hi, lo = split(rows_ref[...].reshape(blocks * rows, depth))
    for n in range(0, out_ref.shape[2], 256):
        dot = lambda a, b: jnp.dot(a, b[:, n : n + 256], preferred_element_type=F32)
        acc = dot(lo, sh_ref) + dot(hi, sl_ref) + dot(hi, sh_ref)
        for b in range(blocks):
            out_ref[tab_ref[step * blocks + b], :, n : n + 256] = acc[b * rows : (b + 1) * rows]


def whole_products(tab, gathered, sigma):
    blocks, rows, depth = gathered.shape
    width = sigma[0].shape[1]
    group = 8
    whole = pl.BlockSpec(sigma[0].shape, lambda i: (0, 0))
    return pl.pallas_call(
        whole_kernel,
        grid=(blocks // group,),
        in_specs=[
            pl.BlockSpec(memory_space=pltpu.SMEM),
            pl.BlockSpec((group, rows, depth), lambda i: (i, 0, 0)),
            whole,
            whole,
        ],
        out_specs=pl.BlockSpec((blocks, rows, width), lambda i: (0, 0, 0)),
        out_shape=jax.ShapeDtypeStruct((blocks, rows, width), F32),
        compiler_params=pltpu.CompilerParams(vmem_limit_bytes=40 * 2**20),
        cost_estimate=pl.CostEstimate(
            flops=6 * blocks * rows * depth * width,
            bytes_accessed=blocks * rows * depth * 4 + 2**23,
            transcendentals=0,
        ),
        name="whole_products",
    )(tab, gathered, *sigma)


def turn_kernel(core_ref, own_ref, recv_ref, high_ref, low_ref):
    n = own_ref.shape[1]
    for at, ref in ((0, own_ref), (n, recv_ref)):
        high_ref[at : at + n, :], low_ref[at : at + n, :] = split(ref[...].T)


def turn_both(core, sigma, recv):
    rows, n = recv.shape
    steps = rows // 256
    return pl.pallas_call(
        turn_kernel,
        grid_spec=pltpu.PrefetchScalarGridSpec(
            num_scalar_prefetch=1,
            grid=(steps,),
            in_specs=[
                pl.BlockSpec((256, n), lambda i, core: (i + core[0] * steps, 0)),
                pl.BlockSpec((256, n), lambda i, core: (i, 0)),
            ],
            out_specs=[pl.BlockSpec((2 * n, 256), lambda i, core: (0, i))] * 2,
        ),
        out_shape=[jax.ShapeDtypeStruct((2 * n, rows), BF16)] * 2,
        name="turn_sigma",
    )(core, sigma, recv)


def turned_kernel(tab_ref, own_ref, recv_ref, sh_ref, sl_ref, *refs):
    outs, rows_ref = refs[:-1], refs[-1]
    blocks, rows, n = own_ref.shape
    for side, ref in ((0, own_ref), (1, recv_ref)):
        for b in range(blocks):
            at = pl.ds(pl.multiple_of(tab_ref[side, b] * rows, rows), rows)
            rows_ref[at, side * n : side * n + n] = ref[b]
    hi, lo = split(rows_ref[...])
    for c in range(0, sh_ref.shape[1], 256):
        columns = slice(c, c + 256)
        dot = lambda a, b: jnp.dot(a, b[:, columns], preferred_element_type=F32)
        acc = dot(lo, sh_ref) + dot(hi, sl_ref) + dot(hi, sh_ref)
        at = 0
        for out in outs:
            for b in range(out.shape[0]):
                out[b, :, columns] = acc[at : at + rows]
                at += rows


def turned_products(tab, own, recv, sigmas):
    blocks, rows, n = own.shape
    vmem = pl.BlockSpec(memory_space=pltpu.VMEM)
    total = blocks * rows
    width = sigmas[0].shape[1]
    return pl.pallas_call(
        turned_kernel,
        in_specs=[pl.BlockSpec(memory_space=pltpu.SMEM)] + [vmem] * 4,
        out_specs=[vmem] * 5,
        out_shape=[jax.ShapeDtypeStruct((n, rows, width), F32) for n in (8, 8, 4, 4, 8)],
        scratch_shapes=[pltpu.VMEM((total, 2 * n), F32)],
        compiler_params=pltpu.CompilerParams(vmem_limit_bytes=40 * 2**20),
        cost_estimate=pl.CostEstimate(
            flops=6 * total * 2 * n * width, bytes_accessed=total * 8192 + 2**22, transcendentals=0
        ),
        name="turned_products",
    )(tab, own, recv, *sigmas)


def final_kernel(shift_ref, mask_ref, masked_ref, *refs):
    blocks, halves, (off_ref, var_ref) = refs[:4], refs[4:6], refs[6:]
    at = 0
    for pieces, places, width in ((blocks, (0, 1, 2, 3), 512), (halves, (4, 5), 1024)):
        rows = pieces[0].shape[0]
        total = jnp.zeros((rows, 128), F32)
        for piece, k in zip(pieces, places):
            columns = pl.ds(pl.multiple_of(shift_ref[k] * width, width), width)
            product = piece[...]
            off_ref[at : at + rows, columns] = -(product * mask_ref[:, columns])
            part = product * masked_ref[at : at + rows, columns]
            for n in range(0, width, 128):
                total += part[:, n : n + 128]
        var_ref[at : at + rows, :] = total
        at += rows


def finish(shift, mask, masked, groups):
    vmem = pl.BlockSpec(memory_space=pltpu.VMEM)
    return pl.pallas_call(
        final_kernel,
        in_specs=[pl.BlockSpec(memory_space=pltpu.SMEM)] + [vmem] * (2 + len(groups)),
        out_specs=[vmem] * 2,
        out_shape=[
            jax.ShapeDtypeStruct(masked.shape, F32),
            jax.ShapeDtypeStruct((masked.shape[0], 128), F32),
        ],
        name="finish",
    )(shift, mask, masked, *groups)


def places(row, col):
    zh, y, zl, x, core = row // 4, row % 4, col // 8, (col // 2) % 4, col % 2
    c = jnp.arange(32, dtype=jnp.int32)
    s, i = c // 4, c % 4
    whole = (s % 4) * 8 + ((s // 4) ^ zh) * 4 + (i - col) % 4
    d, e, k = c // 8, (c // 4) % 2, c % 4
    s = (zh ^ e) * 4 + (y - d) % 4
    tabs = []
    for c in (col, col ^ 1):
        i = (c - k) % 4
        to_zl, to_x, to_core = s // 2, 2 * (s % 2) + i // 2, i % 2
        tabs.append(((to_x - x) % 4) * 8 + ((to_zl - zl) % 4) * 2 + (to_core ^ core))
    return whole, jnp.stack(tabs)


def body(sigma_anc, factor, pattern, base_var):
    row, col = lax.axis_index("row"), lax.axis_index("col")
    core = col % 2
    whole_tab, turned_tab = places(row, col)
    half = 1024
    blocks = lax.dynamic_slice(pattern, (col // 4, row * 8), (1, 8)).astype(F32)
    mask = jnp.repeat(blocks, B, axis=1)
    masked = factor * mask

    gathered = lax.all_gather(masked[:FIRST], "col")

    rest = masked[FIRST:]
    rows = rest.shape[0]
    quarters = [
        send(lax.dynamic_slice(rest, (0, 512 * ((col + n) % 4)), (rows, 512)), regroup(n))
        for n in range(4)
    ]
    own = to_other_zh(jnp.stack(quarters))
    own, sigma_anc = tie(own, sigma_anc)
    own = jnp.concatenate([own] + [send(own, along_y(n)) for n in (1, 2, 3)])
    sigma_other = lax.dynamic_slice(sigma_anc, ((1 - core) * half, 0), (half, 512))
    sigma = split_all(sigma_anc)
    turned = turn_both(core[None], sigma_anc, send(sigma_other, OTHER_CORE))
    own, sigma, turned = tie(own, sigma, turned)
    recv = send(own, OTHER_CORE)

    first = whole_products(whole_tab, gathered, sigma)
    first, recv = tie(first, recv)
    here, right, far_right, far_left, left = turned_products(turned_tab, own, recv, turned)
    pairs = [[0, 1, 2, 3], [4, 5, 6, 7]]
    first = lax.psum_scatter(first, "row", scatter_dimension=0, axis_index_groups=pairs, tiled=True)

    right = jnp.concatenate([right[:4] + send(far_right, along_x(1)), right[4:]])
    left = jnp.concatenate([left[:4], left[4:] + send(far_left, along_x(-1))])
    here = here + send(right, along_x(1)) + send(left, along_x(-1))
    first = sum_zh(first)
    here, first = tie(here, first)
    groups = [send(first[n], regroup(n)) for n in range(4)]
    total = here[:2]
    for n in (1, 2, 3):
        total = total + send(here[2 * n : 2 * n + 2], along_zl(n))
    *groups, total = tie(*groups, total)
    groups += [total[0], send(total[1], OTHER_CORE)]

    shift = jnp.concatenate([(col - jnp.arange(4, dtype=jnp.int32)) % 4, jnp.stack([core, 1 - core])])
    sigma_off, var_lanes = finish(shift, mask, masked, groups)
    part = jnp.sum(var_lanes, axis=1)
    shares = jnp.broadcast_to(part[None, :], (8, part.shape[0]))
    shares = lax.all_to_all(shares, "row", 0, 0, tiled=True)
    return sigma_off, base_var + jnp.sum(shares, axis=0)


def to_other_zh(part):
    return jnp.concatenate([part, send(part, OTHER_ZH)])


def sum_zh(part):
    return part[:4] + send(part[4:], OTHER_ZH)


def solution(mesh):
    in_specs = (P("row", "col"), P("col", "row"), P(), P("col"))
    out_specs = (P("col", "row"), P("col"))
    return jax.shard_map(body, mesh=mesh, in_specs=in_specs, out_specs=out_specs, check_vma=False)
```

```python
import jax
import jax.numpy as jnp
from jax import lax
from jax.experimental import pallas as pl
from jax.experimental.pallas import tpu as pltpu
from jax.sharding import PartitionSpec as P

B = 256
AXES = ("row", "col")
FIRST = 40
F32, BF16 = jnp.float32, jnp.bfloat16


def table(move):
    perm = []
    for i in range(256):
        zh, y, zl, x, k = i >> 7, (i >> 5) & 3, (i >> 3) & 3, (i >> 1) & 3, i & 1
        zh, y, zl, x, k = move(zh, y, zl, x, k)
        perm.append((i, (zh << 7) | ((y % 4) << 5) | ((zl % 4) << 3) | ((x % 4) << 1) | k))
    return perm


def along_x(n):
    return table(lambda zh, y, zl, x, k: (zh, y, zl, x + n, k))


def along_y(n):
    return table(lambda zh, y, zl, x, k: (zh, y + n, zl, x, k))


def along_zl(n):
    return table(lambda zh, y, zl, x, k: (zh, y, zl + n, x, k))


OTHER_ZH = table(lambda zh, y, zl, x, k: (1 - zh, y, zl, x, k))
OTHER_CORE = table(lambda zh, y, zl, x, k: (zh, y, zl, x, 1 - k))


def regroup(n):
    perm = []
    for i in range(256):
        r, c = i >> 5, i & 31
        perm.append((i, (c // 4) * 32 + 4 * r + (c + n) % 4))
    return perm


def send(value, perm):
    return lax.ppermute(value, AXES, perm)


def tie(*values):
    return lax.optimization_barrier(values)


def split(value):
    high = value.astype(BF16)
    return high, (value - high.astype(F32)).astype(BF16)


def split_kernel(value_ref, high_ref, low_ref):
    high_ref[...], low_ref[...] = split(value_ref[...])


def split_all(value):
    spec = pl.BlockSpec((256, value.shape[1]), lambda i: (i, 0))
    return pl.pallas_call(
        split_kernel,
        grid=(value.shape[0] // 256,),
        in_specs=[spec],
        out_specs=[spec] * 2,
        out_shape=[jax.ShapeDtypeStruct(value.shape, BF16)] * 2,
        name="split_sigma",
    )(value)


def whole_kernel(tab_ref, rows_ref, sh_ref, sl_ref, out_ref):
    step = pl.program_id(0)
    blocks, rows, depth = rows_ref.shape
    hi, lo = split(rows_ref[...].reshape(blocks * rows, depth))
    both, count = jnp.concatenate([hi, lo]), hi.shape[0]
    for n in range(0, out_ref.shape[2], 256):
        dot = lambda a, b: jnp.dot(a, b[:, n : n + 256], preferred_element_type=F32)
        acc = dot(both, sh_ref)
        acc = acc[:count] + acc[count:] + dot(hi, sl_ref)
        for b in range(blocks):
            out_ref[tab_ref[step * blocks + b], :, n : n + 256] = acc[b * rows : (b + 1) * rows]


def whole_products(tab, gathered, sigma):
    blocks, rows, depth = gathered.shape
    width = sigma[0].shape[1]
    group = 8
    whole = pl.BlockSpec(sigma[0].shape, lambda i: (0, 0))
    return pl.pallas_call(
        whole_kernel,
        grid=(blocks // group,),
        in_specs=[
            pl.BlockSpec(memory_space=pltpu.SMEM),
            pl.BlockSpec((group, rows, depth), lambda i: (i, 0, 0)),
            whole,
            whole,
        ],
        out_specs=pl.BlockSpec((blocks, rows, width), lambda i: (0, 0, 0)),
        out_shape=jax.ShapeDtypeStruct((blocks, rows, width), F32),
        compiler_params=pltpu.CompilerParams(vmem_limit_bytes=60 * 2**20),
        cost_estimate=pl.CostEstimate(
            flops=6 * blocks * rows * depth * width,
            bytes_accessed=blocks * rows * depth * 4 + 2**23,
            transcendentals=0,
        ),
        name="whole_products",
    )(tab, gathered, *sigma)


def turn_kernel(core_ref, own_ref, recv_ref, high_ref, low_ref):
    n = own_ref.shape[1]
    for at, ref in ((0, own_ref), (n, recv_ref)):
        high_ref[at : at + n, :], low_ref[at : at + n, :] = split(ref[...].T)


def turn_both(core, sigma, recv):
    rows, n = recv.shape
    steps = rows // 256
    return pl.pallas_call(
        turn_kernel,
        grid_spec=pltpu.PrefetchScalarGridSpec(
            num_scalar_prefetch=1,
            grid=(steps,),
            in_specs=[
                pl.BlockSpec((256, n), lambda i, core: (i + core[0] * steps, 0)),
                pl.BlockSpec((256, n), lambda i, core: (i, 0)),
            ],
            out_specs=[pl.BlockSpec((2 * n, 256), lambda i, core: (0, i))] * 2,
        ),
        out_shape=[jax.ShapeDtypeStruct((2 * n, rows), BF16)] * 2,
        name="turn_sigma",
    )(core, sigma, recv)


def turned_kernel(tab_ref, own_ref, recv_ref, sh_ref, sl_ref, *refs):
    outs, rows_ref = refs[:-1], refs[-1]
    blocks, rows, n = own_ref.shape
    for side, ref in ((0, own_ref), (1, recv_ref)):
        for b in range(blocks):
            at = pl.ds(pl.multiple_of(tab_ref[side, b] * rows, rows), rows)
            rows_ref[at, side * n : side * n + n] = ref[b]
    hi, lo = split(rows_ref[...])
    both, count = jnp.concatenate([hi, lo]), hi.shape[0]
    for c in range(0, sh_ref.shape[1], 256):
        columns = slice(c, c + 256)
        dot = lambda a, b: jnp.dot(a, b[:, columns], preferred_element_type=F32)
        acc = dot(both, sh_ref)
        acc = acc[:count] + acc[count:] + dot(hi, sl_ref)
        at = 0
        for out in outs:
            for b in range(out.shape[0]):
                out[b, :, columns] = acc[at : at + rows]
                at += rows


def turned_products(tab, own, recv, sigmas):
    blocks, rows, n = own.shape
    vmem = pl.BlockSpec(memory_space=pltpu.VMEM)
    total = blocks * rows
    width = sigmas[0].shape[1]
    return pl.pallas_call(
        turned_kernel,
        in_specs=[pl.BlockSpec(memory_space=pltpu.SMEM)] + [vmem] * 4,
        out_specs=[vmem] * 5,
        out_shape=[jax.ShapeDtypeStruct((n, rows, width), F32) for n in (8, 8, 4, 4, 8)],
        scratch_shapes=[pltpu.VMEM((total, 2 * n), F32)],
        compiler_params=pltpu.CompilerParams(vmem_limit_bytes=60 * 2**20),
        cost_estimate=pl.CostEstimate(
            flops=6 * total * 2 * n * width, bytes_accessed=total * 8192 + 2**22, transcendentals=0
        ),
        name="turned_products",
    )(tab, own, recv, *sigmas)


def final_kernel(shift_ref, mask_ref, masked_ref, *refs):
    blocks, halves, (off_ref, var_ref) = refs[:4], refs[4:6], refs[6:]
    at, sums = 0, []
    for pieces, places, width in ((blocks, (0, 1, 2, 3), 512), (halves, (4, 5), 1024)):
        rows = pieces[0].shape[0]
        total = jnp.zeros((rows, 128), F32)
        for piece, k in zip(pieces, places):
            columns = pl.ds(pl.multiple_of(shift_ref[k] * width, width), width)
            product = piece[...]
            off_ref[at : at + rows, columns] = -(product * mask_ref[:, columns])
            part = product * masked_ref[at : at + rows, columns]
            for n in range(0, width, 128):
                total += part[:, n : n + 128]
        sums.append(total)
        at += rows
    sums = jnp.concatenate(sums)
    var_ref[...] = lax.dot_general(
        jnp.ones((8, 128), F32),
        sums,
        (((1,), (1,)), ((), ())),
        precision=lax.Precision.HIGHEST,
        preferred_element_type=F32,
    )


def finish(shift, mask, masked, groups):
    vmem = pl.BlockSpec(memory_space=pltpu.VMEM)
    return pl.pallas_call(
        final_kernel,
        in_specs=[pl.BlockSpec(memory_space=pltpu.SMEM)] + [vmem] * (2 + len(groups)),
        out_specs=[vmem] * 2,
        out_shape=[
            jax.ShapeDtypeStruct(masked.shape, F32),
            jax.ShapeDtypeStruct((8, masked.shape[0]), F32),
        ],
        name="finish",
    )(shift, mask, masked, *groups)


def places(row, col):
    zh, y, zl, x, core = row // 4, row % 4, col // 8, (col // 2) % 4, col % 2
    c = jnp.arange(32, dtype=jnp.int32)
    s, i = c // 4, c % 4
    whole = (s % 4) * 8 + ((s // 4) ^ zh) * 4 + (i - col) % 4
    d, e, k = c // 8, (c // 4) % 2, c % 4
    s = (zh ^ e) * 4 + (y - d) % 4
    tabs = []
    for c in (col, col ^ 1):
        i = (c - k) % 4
        to_zl, to_x, to_core = s // 2, 2 * (s % 2) + i // 2, i % 2
        tabs.append(((to_x - x) % 4) * 8 + ((to_zl - zl) % 4) * 2 + (to_core ^ core))
    return whole, jnp.stack(tabs)


def body(sigma_anc, factor, pattern, base_var):
    row, col = lax.axis_index("row"), lax.axis_index("col")
    core = col % 2
    whole_tab, turned_tab = places(row, col)
    half = 1024
    blocks = lax.dynamic_slice(pattern, (col // 4, row * 8), (1, 8)).astype(F32)
    mask = jnp.repeat(blocks, B, axis=1)
    masked = factor * mask

    gathered = lax.all_gather(masked[:FIRST], "col")

    rest = masked[FIRST:]
    rows = rest.shape[0]
    quarters = [
        send(lax.dynamic_slice(rest, (0, 512 * ((col + n) % 4)), (rows, 512)), regroup(n))
        for n in range(4)
    ]
    own = to_other_zh(jnp.stack(quarters))
    own, sigma_anc = tie(own, sigma_anc)
    own = jnp.concatenate([own] + [send(own, along_y(n)) for n in (1, 2, 3)])
    sigma_other = lax.dynamic_slice(sigma_anc, ((1 - core) * half, 0), (half, 512))
    sigma = split_all(sigma_anc)
    turned = turn_both(core[None], sigma_anc, send(sigma_other, OTHER_CORE))
    own, sigma, turned = tie(own, sigma, turned)
    recv = send(own, OTHER_CORE)

    first = whole_products(whole_tab, gathered, sigma)
    first, recv = tie(first, recv)
    here, right, far_right, far_left, left = turned_products(turned_tab, own, recv, turned)
    pairs = [[0, 1, 2, 3], [4, 5, 6, 7]]
    first = lax.psum_scatter(first, "row", scatter_dimension=0, axis_index_groups=pairs, tiled=True)

    right = jnp.concatenate([right[:4] + send(far_right, along_x(1)), right[4:]])
    left = jnp.concatenate([left[:4], left[4:] + send(far_left, along_x(-1))])
    here = here + send(right, along_x(1)) + send(left, along_x(-1))
    first = sum_zh(first)
    groups = [send(first[n], regroup(n)) for n in range(4)]
    total = here[:2]
    for n in (1, 2, 3):
        total = total + send(here[2 * n : 2 * n + 2], along_zl(n))
    *groups, total = tie(*groups, total)
    groups += [total[0], send(total[1], OTHER_CORE)]

    shift = jnp.concatenate([(col - jnp.arange(4, dtype=jnp.int32)) % 4, jnp.stack([core, 1 - core])])
    sigma_off, shares = finish(shift, mask, masked, groups)
    shares = lax.all_to_all(shares, "row", 0, 0, tiled=True)
    return sigma_off, base_var + jnp.sum(shares, axis=0)


def to_other_zh(part):
    return jnp.concatenate([part, send(part, OTHER_ZH)])


def sum_zh(part):
    return part[:4] + send(part[4:], OTHER_ZH)


def solution(mesh):
    in_specs = (P("row", "col"), P("col", "row"), P(), P("col"))
    out_specs = (P("col", "row"), P("col"))
    return jax.shard_map(body, mesh=mesh, in_specs=in_specs, out_specs=out_specs, check_vma=False)
```

```python
import jax
import jax.numpy as jnp
from jax import lax
from jax.experimental import pallas as pl
from jax.experimental.pallas import tpu as pltpu
from jax.sharding import PartitionSpec as P

B = 256
AXES = ("row", "col")
FIRST = 40
F32, BF16 = jnp.float32, jnp.bfloat16


def table(move):
    perm = []
    for i in range(256):
        zh, y, zl, x, k = i >> 7, (i >> 5) & 3, (i >> 3) & 3, (i >> 1) & 3, i & 1
        zh, y, zl, x, k = move(zh, y, zl, x, k)
        perm.append((i, (zh << 7) | ((y % 4) << 5) | ((zl % 4) << 3) | ((x % 4) << 1) | k))
    return perm


def along_x(n):
    return table(lambda zh, y, zl, x, k: (zh, y, zl, x + n, k))


def along_y(n):
    return table(lambda zh, y, zl, x, k: (zh, y + n, zl, x, k))


def along_zl(n):
    return table(lambda zh, y, zl, x, k: (zh, y, zl + n, x, k))


OTHER_ZH = table(lambda zh, y, zl, x, k: (1 - zh, y, zl, x, k))
OTHER_CORE = table(lambda zh, y, zl, x, k: (zh, y, zl, x, 1 - k))


def regroup(n):
    perm = []
    for i in range(256):
        r, c = i >> 5, i & 31
        perm.append((i, (c // 4) * 32 + 4 * r + (c + n) % 4))
    return perm


def send(value, perm):
    return lax.ppermute(value, AXES, perm)


def tie(*values):
    return lax.optimization_barrier(values)


def split(value):
    high = value.astype(BF16)
    return high, (value - high.astype(F32)).astype(BF16)


def split_kernel(value_ref, high_ref, low_ref):
    high_ref[...], low_ref[...] = split(value_ref[...])


def split_all(value):
    spec = pl.BlockSpec((256, value.shape[1]), lambda i: (i, 0))
    return pl.pallas_call(
        split_kernel,
        grid=(value.shape[0] // 256,),
        in_specs=[spec],
        out_specs=[spec] * 2,
        out_shape=[jax.ShapeDtypeStruct(value.shape, BF16)] * 2,
        name="split_sigma",
    )(value)


def whole_kernel(tab_ref, rows_ref, sh_ref, sl_ref, out_ref):
    step = pl.program_id(0)
    blocks, rows, depth = rows_ref.shape
    hi, lo = split(rows_ref[...].reshape(blocks * rows, depth))
    both, count = jnp.concatenate([hi, lo]), hi.shape[0]
    for n in range(0, out_ref.shape[2], 256):
        dot = lambda a, b: jnp.dot(a, b[:, n : n + 256], preferred_element_type=F32)
        acc = dot(both, sh_ref)
        acc = acc[:count] + acc[count:] + dot(hi, sl_ref)
        for b in range(blocks):
            out_ref[tab_ref[step * blocks + b], :, n : n + 256] = acc[b * rows : (b + 1) * rows]


def whole_products(tab, gathered, sigma):
    blocks, rows, depth = gathered.shape
    width = sigma[0].shape[1]
    group = 8
    whole = pl.BlockSpec(sigma[0].shape, lambda i: (0, 0))
    return pl.pallas_call(
        whole_kernel,
        grid=(blocks // group,),
        in_specs=[
            pl.BlockSpec(memory_space=pltpu.SMEM),
            pl.BlockSpec((group, rows, depth), lambda i: (i, 0, 0)),
            whole,
            whole,
        ],
        out_specs=pl.BlockSpec((blocks, rows, width), lambda i: (0, 0, 0)),
        out_shape=jax.ShapeDtypeStruct((blocks, rows, width), F32),
        compiler_params=pltpu.CompilerParams(vmem_limit_bytes=60 * 2**20),
        cost_estimate=pl.CostEstimate(
            flops=6 * blocks * rows * depth * width,
            bytes_accessed=blocks * rows * depth * 4 + 2**23,
            transcendentals=0,
        ),
        name="whole_products",
    )(tab, gathered, *sigma)


def turn_kernel(core_ref, own_ref, recv_ref, high_ref, low_ref):
    n = own_ref.shape[1]
    for at, ref in ((0, own_ref), (n, recv_ref)):
        high_ref[at : at + n, :], low_ref[at : at + n, :] = split(ref[...].T)


def turn_both(core, sigma, recv):
    rows, n = recv.shape
    steps = rows // 256
    return pl.pallas_call(
        turn_kernel,
        grid_spec=pltpu.PrefetchScalarGridSpec(
            num_scalar_prefetch=1,
            grid=(steps,),
            in_specs=[
                pl.BlockSpec((256, n), lambda i, core: (i + core[0] * steps, 0)),
                pl.BlockSpec((256, n), lambda i, core: (i, 0)),
            ],
            out_specs=[pl.BlockSpec((2 * n, 256), lambda i, core: (0, i))] * 2,
        ),
        out_shape=[jax.ShapeDtypeStruct((2 * n, rows), BF16)] * 2,
        name="turn_sigma",
    )(core, sigma, recv)


def turned_kernel(tab_ref, own_ref, recv_ref, sh_ref, sl_ref, *refs):
    outs, rows_ref = refs[:-1], refs[-1]
    blocks, rows, n = own_ref.shape
    for side, ref in ((0, own_ref), (1, recv_ref)):
        for b in range(blocks):
            at = pl.ds(pl.multiple_of(tab_ref[side, b] * rows, rows), rows)
            rows_ref[at, side * n : side * n + n] = ref[b]
    hi, lo = split(rows_ref[...])
    both, count = jnp.concatenate([hi, lo]), hi.shape[0]
    for c in range(0, sh_ref.shape[1], 256):
        columns = slice(c, c + 256)
        dot = lambda a, b: jnp.dot(a, b[:, columns], preferred_element_type=F32)
        acc = dot(both, sh_ref)
        acc = acc[:count] + acc[count:] + dot(hi, sl_ref)
        at = 0
        for out in outs:
            for b in range(out.shape[0]):
                out[b, :, columns] = acc[at : at + rows]
                at += rows


def turned_products(tab, own, recv, sigmas):
    blocks, rows, n = own.shape
    vmem = pl.BlockSpec(memory_space=pltpu.VMEM)
    total = blocks * rows
    width = sigmas[0].shape[1]
    return pl.pallas_call(
        turned_kernel,
        in_specs=[pl.BlockSpec(memory_space=pltpu.SMEM)] + [vmem] * 4,
        out_specs=[vmem] * 5,
        out_shape=[jax.ShapeDtypeStruct((n, rows, width), F32) for n in (8, 8, 4, 4, 8)],
        scratch_shapes=[pltpu.VMEM((total, 2 * n), F32)],
        compiler_params=pltpu.CompilerParams(vmem_limit_bytes=60 * 2**20),
        cost_estimate=pl.CostEstimate(
            flops=6 * total * 2 * n * width, bytes_accessed=total * 8192 + 2**22, transcendentals=0
        ),
        name="turned_products",
    )(tab, own, recv, *sigmas)


def final_kernel(shift_ref, mask_ref, masked_ref, *refs):
    blocks, halves, (off_ref, var_ref) = refs[:4], refs[4:6], refs[6:]
    at, sums = 0, []
    for pieces, places, width in ((blocks, (0, 1, 2, 3), 512), (halves, (4, 5), 1024)):
        rows = pieces[0].shape[0]
        total = jnp.zeros((rows, 128), F32)
        for piece, k in zip(pieces, places):
            columns = pl.ds(pl.multiple_of(shift_ref[k] * width, width), width)
            product = piece[...]
            off_ref[at : at + rows, columns] = -(product * mask_ref[:, columns])
            part = product * masked_ref[at : at + rows, columns]
            for n in range(0, width, 128):
                total += part[:, n : n + 128]
        sums.append(total)
        at += rows
    sums = jnp.concatenate(sums)
    var_ref[...] = lax.dot_general(
        jnp.ones((8, 128), F32),
        sums,
        (((1,), (1,)), ((), ())),
        precision=lax.Precision.HIGHEST,
        preferred_element_type=F32,
    )


def finish(shift, mask, masked, groups):
    vmem = pl.BlockSpec(memory_space=pltpu.VMEM)
    return pl.pallas_call(
        final_kernel,
        in_specs=[pl.BlockSpec(memory_space=pltpu.SMEM)] + [vmem] * (2 + len(groups)),
        out_specs=[vmem] * 2,
        out_shape=[
            jax.ShapeDtypeStruct(masked.shape, F32),
            jax.ShapeDtypeStruct((8, masked.shape[0]), F32),
        ],
        name="finish",
    )(shift, mask, masked, *groups)


def places(row, col):
    zh, y, zl, x, core = row // 4, row % 4, col // 8, (col // 2) % 4, col % 2
    c = jnp.arange(32, dtype=jnp.int32)
    s, i = c // 4, c % 4
    whole = (s % 4) * 8 + ((s // 4) ^ zh) * 4 + (i - col) % 4
    d, e, k = c // 8, (c // 4) % 2, c % 4
    s = (zh ^ e) * 4 + (y - d) % 4
    tabs = []
    for c in (col, col ^ 1):
        i = (c - k) % 4
        to_zl, to_x, to_core = s // 2, 2 * (s % 2) + i // 2, i % 2
        tabs.append(((to_x - x) % 4) * 8 + ((to_zl - zl) % 4) * 2 + (to_core ^ core))
    return whole, jnp.stack(tabs)


def body(sigma_anc, factor, pattern, base_var):
    row, col = lax.axis_index("row"), lax.axis_index("col")
    core = col % 2
    whole_tab, turned_tab = places(row, col)
    half = 1024
    blocks = lax.dynamic_slice(pattern, (col // 4, row * 8), (1, 8)).astype(F32)
    mask = jnp.repeat(blocks, B, axis=1)
    masked = factor * mask

    gathered = lax.all_gather(factor[:FIRST] * mask, "col")

    rest = masked[FIRST:]
    rows = rest.shape[0]
    quarters = [
        send(lax.dynamic_slice(rest, (0, 512 * ((col + n) % 4)), (rows, 512)), regroup(n))
        for n in range(4)
    ]
    own = to_other_zh(jnp.stack(quarters))
    own, sigma_anc = tie(own, sigma_anc)
    own = jnp.concatenate([own] + [send(own, along_y(n)) for n in (1, 2, 3)])
    sigma_other = lax.dynamic_slice(sigma_anc, ((1 - core) * half, 0), (half, 512))
    sigma = split_all(sigma_anc)
    turned = turn_both(core[None], sigma_anc, send(sigma_other, OTHER_CORE))
    own, sigma, turned = tie(own, sigma, turned)
    recv = send(own, OTHER_CORE)

    first = whole_products(whole_tab, gathered, sigma)
    first, recv = tie(first, recv)
    here, right, far_right, far_left, left = turned_products(turned_tab, own, recv, turned)
    pairs = [[0, 1, 2, 3], [4, 5, 6, 7]]
    first = lax.psum_scatter(first, "row", scatter_dimension=0, axis_index_groups=pairs, tiled=True)

    right = jnp.concatenate([right[:4] + send(far_right, along_x(1)), right[4:]])
    left = jnp.concatenate([left[:4], left[4:] + send(far_left, along_x(-1))])
    here = here + send(right, along_x(1)) + send(left, along_x(-1))
    shift = jnp.concatenate([(col - jnp.arange(4, dtype=jnp.int32)) % 4, jnp.stack([core, 1 - core])])
    first, shift = tie(first, shift)
    first = sum_zh(first)
    groups = [send(first[n], regroup(n)) for n in range(4)]
    total = here[:2]
    for n in (1, 2, 3):
        total = total + send(here[2 * n : 2 * n + 2], along_zl(n))
    groups[3], total = tie(groups[3], total)
    groups += [total[0], send(total[1], OTHER_CORE)]

    sigma_off, shares = finish(shift, mask, masked, groups)
    shares = lax.all_to_all(shares, "row", 0, 0, tiled=True)
    return sigma_off, base_var + jnp.sum(shares, axis=0)


def to_other_zh(part):
    return jnp.concatenate([part, send(part, OTHER_ZH)])


def sum_zh(part):
    return part[:4] + send(part[4:], OTHER_ZH)


def solution(mesh):
    in_specs = (P("row", "col"), P("col", "row"), P(), P("col"))
    out_specs = (P("col", "row"), P("col"))
    return jax.shard_map(body, mesh=mesh, in_specs=in_specs, out_specs=out_specs, check_vma=False)
```
